32 devices in a mesh: grp: 4 (over x, core), dev: 8 (over z, y).
Axes of the slice: x: 2, y: 2, z: 4, core: 2. Of those that a mesh axis runs over, the one named last changes fastest.
Arguments:
- tensor_slab: bfloat16 [512, 512, 32, 64], P(None, 'dev', 'grp'), may hold values from -400 to 400
- mode_factor: bfloat16 [512, 64], replicated, may hold values from -40 to 40
Outputs:
- triangle: float32 [512, 512], P('dev', 'grp')
The draws below stay inside these ranges and needn't reach their ends.
All inputs are finite; a program needn't handle non-finite values.
Results may differ from the reference program's by a relative error of at most 0.00033.
Values may be sent and summed in bfloat16 or wider, within the bound.
No kernel may reach another device: no remote copies, remote signals or barrier semaphores. Data moves between devices by JAX's collectives and lax.ppermute only.
A program may use at most 64 MiB of HBM per device.

```python
import jax
import jax.numpy as jnp
from jax import lax

N1 = 512
N2 = 512
R1 = 64
S = 64
NZ = 32
ROWS = 131072


def draw_tensor_slab(key, part):
    key_list = jax.random.split(jax.random.fold_in(key, 11), 6)
    noise = jnp.clip(jax.random.normal(key_list[0], (N1, N2, NZ, S), jnp.float32), -6.0, 6.0)
    common = jnp.clip(jax.random.normal(key_list[1], (N1, 1, NZ, S), jnp.float32), -6.0, 6.0)
    loading = jnp.clip(0.7 * jax.random.normal(key_list[2], (N2,), jnp.float32), -2.0, 2.0)
    column_scale = jnp.exp(jax.random.uniform(key_list[3], (N2,), jnp.float32, jnp.log(0.3), jnp.log(3.0)))
    depth_scale = (1.0 + 2.0 * jnp.arange(NZ, dtype=jnp.float32) / NZ) * jnp.exp(jax.random.uniform(key_list[4], (NZ,), jnp.float32, jnp.log(0.5), jnp.log(2.0)))
    species_scale = jnp.exp(jax.random.uniform(key_list[5], (S,), jnp.float32, jnp.log(0.5), jnp.log(2.0)))
    values = column_scale[None, :, None, None] * (noise + loading[None, :, None, None] * common)
    values = values * depth_scale[None, None, :, None] * species_scale[None, None, None, :]
    return values.astype(jnp.bfloat16)


def draw_mode_factor(key, part):
    key_list = jax.random.split(jax.random.fold_in(key, 23), 2)
    entries = jnp.clip(jax.random.normal(key_list[0], (N1, R1), jnp.float32), -6.0, 6.0)
    rank_scale = (1.0 + 2.0 * jnp.arange(R1, dtype=jnp.float32) / R1) * jnp.exp(jax.random.uniform(key_list[1], (R1,), jnp.float32, jnp.log(0.5), jnp.log(2.0)))
    return (entries * rank_scale[None, :] / jnp.sqrt(jnp.float32(N1))).astype(jnp.bfloat16)


def setup_inputs(seed: int = 0) -> dict:
    streams_of = jax.random.split(jax.random.key(seed), 3)
    return {
        "tensor_slab": draw_tensor_slab(jax.random.fold_in(streams_of[2], 71), 0),
        "mode_factor": draw_mode_factor(jax.random.fold_in(streams_of[2], 71), 0),
    }


def reference(tensor_slab, mode_factor):
    factor_wide = mode_factor.astype(jnp.float32)

    def absorb(running, slab_index):
        slab_piece = lax.dynamic_index_in_dim(tensor_slab, slab_index, 2, keepdims=False).astype(jnp.float32)
        projected = jnp.einsum('ir,ijs->rsj', factor_wide, slab_piece, precision=lax.Precision.HIGHEST)
        projected = projected.astype(jnp.bfloat16).reshape(R1 * S, N2)
        return (running + jnp.dot(projected.T.astype(jnp.float32), projected.astype(jnp.float32), preferred_element_type=jnp.float32), None)
    gram_total, unused_out = lax.scan(absorb, jnp.zeros((N2, N2), jnp.float32), jnp.arange(NZ, dtype=jnp.int32))
    lower_tri = jnp.linalg.cholesky(gram_total / ROWS)
    return lower_tri.T
```

```python
import functools

import jax
import jax.numpy as jnp
from jax import lax
from jax.experimental import pallas as pl
from jax.experimental.pallas import tpu as pltpu
from jax.sharding import PartitionSpec as P

LANES = 128


def project_kernel(rank, dest_ref, slab_ref, factor_ref, out_ref, wide_ref):
    cols, width, depth = slab_ref.shape
    half = width // 2
    flat = slab_ref[...].reshape(cols * width, depth)
    wide_ref[...] = jnp.dot(flat, factor_ref[...], preferred_element_type=jnp.float32)
    lane = lax.broadcasted_iota(jnp.int32, (cols, LANES), 1)
    for s in range(half):
        low = wide_ref[pl.ds(s, cols, stride=width), :]
        high = wide_ref[pl.ds(s + half, cols, stride=width), :]
        both = jnp.where(lane < rank, low, high)
        out_ref[:, s * LANES:(s + 1) * LANES] = both.astype(out_ref.dtype)


def project(slab, factor_pair, rank, dest, width):
    cols, total_width, depth = slab.shape
    block_cols = 16
    out_width = width * rank
    grid_spec = pltpu.PrefetchScalarGridSpec(
        num_scalar_prefetch=1,
        grid=(cols // block_cols,),
        in_specs=[
            pl.BlockSpec((block_cols, width, depth), lambda c, d: (c, d[0], 0)),
            pl.BlockSpec(factor_pair.shape, lambda c, d: (0, 0)),
        ],
        out_specs=pl.BlockSpec((block_cols, out_width), lambda c, d: (c, 0)),
        scratch_shapes=[pltpu.VMEM((block_cols * width, LANES), jnp.float32)],
    )
    return pl.pallas_call(
        functools.partial(project_kernel, rank),
        out_shape=jax.ShapeDtypeStruct((cols, out_width), jnp.bfloat16),
        grid_spec=grid_spec,
        compiler_params=pltpu.CompilerParams(vmem_limit_bytes=44 * 2**20),
        cost_estimate=pl.CostEstimate(
            flops=8 * cols * width * depth * rank,
            bytes_accessed=2 * cols * width * depth + 2 * cols * out_width,
            transcendentals=0,
        ),
        name="project",
    )(dest.reshape(1), slab, factor_pair)


def lower_blocks(count):
    return [(a, b) for a in range(count) for b in range(a + 1)]


def gram_kernel(scale, count, place_ref, *refs):
    pieces = refs[:count]
    out_ref, full_ref = refs[count:]
    cols = pieces[0].shape[0]
    for i, piece in enumerate(pieces):
        start = pl.multiple_of(place_ref[i] * cols, 16)
        full_ref[pl.ds(start, cols), :] = piece[...]
    order = cols * count
    where = {ab: n for n, ab in enumerate(lower_blocks(order // LANES))}
    wide = 2 * LANES
    for tile in range(order // wide):
        left = full_ref[tile * wide:, :]
        right = full_ref[tile * wide:(tile + 1) * wide, :]
        product = lax.dot_general(
            left, right, (((1,), (1,)), ((), ())), preferred_element_type=jnp.float32
        ) * scale
        for a in range(2 * tile, order // LANES):
            for b in range(2 * tile, min(2 * tile + 2, a + 1)):
                n = where[(a, b)]
                row = (a - 2 * tile) * LANES
                col = (b - 2 * tile) * LANES
                out_ref[n * LANES:(n + 1) * LANES, :] = product[row:row + LANES, col:col + LANES]


def gram(pieces, places, scale):
    cols, width = pieces[0].shape
    count = len(pieces)
    order = cols * count
    rows = len(lower_blocks(order // LANES)) * LANES
    return pl.pallas_call(
        functools.partial(gram_kernel, scale, count),
        out_shape=jax.ShapeDtypeStruct((rows, LANES), jnp.float32),
        in_specs=[pl.BlockSpec(memory_space=pltpu.SMEM)]
        + [pl.BlockSpec(memory_space=pltpu.VMEM)] * count,
        out_specs=pl.BlockSpec(memory_space=pltpu.VMEM),
        scratch_shapes=[pltpu.VMEM((order, width), jnp.bfloat16)],
        compiler_params=pltpu.CompilerParams(vmem_limit_bytes=40 * 2**20),
        cost_estimate=pl.CostEstimate(
            flops=2 * order * order * width,
            bytes_accessed=2 * order * width + 4 * rows * LANES,
            transcendentals=0,
        ),
        name="gram",
    )(places, *pieces)


def reduce_scatter(x, axis):
    n = lax.axis_size(axis)
    shares = x.reshape(n, x.shape[0] // n, LANES)
    return lax.all_to_all(shares, axis, split_axis=0, concat_axis=0, tiled=True).sum(axis=0)


def gather(x, axis):
    n = lax.axis_size(axis)
    copies = jnp.broadcast_to(x[None], (n, *x.shape))
    return lax.all_to_all(copies, axis, split_axis=0, concat_axis=0, tiled=True).reshape(
        n * x.shape[0], LANES
    )


def own_block(full_tri):
    order = full_tri.shape[0]
    row_count = order // lax.axis_size("dev")
    col_count = order // lax.axis_size("grp")
    row_start = lax.axis_index("dev") * row_count
    col_start = lax.axis_index("grp") * col_count
    return lax.dynamic_slice(full_tri, (row_start, col_start), (row_count, col_count))


def per_device(tensor_slab, mode_factor):
    depth, cols, slab_depth, species = tensor_slab.shape
    rank = mode_factor.shape[1]
    n_dev = lax.axis_size("dev")
    n_grp = lax.axis_size("grp")
    me = lax.axis_index("dev")
    slab = tensor_slab.transpose(1, 2, 3, 0).reshape(cols, slab_depth * species, depth)
    width = slab_depth * species // n_dev
    factor_pair = jnp.concatenate([mode_factor, mode_factor], axis=1)
    pieces, places = [], []
    for offset in list(range(n_dev // 2, n_dev)) + list(range(1, n_dev // 2)) + [0]:
        other = jnp.bitwise_xor(me, offset).astype(jnp.int32)
        piece = project(slab, factor_pair, rank, other, width)
        if offset:
            piece = lax.ppermute(piece, "dev", [(i, i ^ offset) for i in range(n_dev)])
        pieces.append(piece)
        places.append(other)
    row_total = rank * slab_depth * species * n_grp
    part = gram(pieces, jnp.stack(places), 1.0 / row_total)
    rows = part.shape[0]
    unit = 8 * n_dev * n_grp
    padded = jnp.pad(part, ((0, -rows % unit), (0, 0)))
    total = reduce_scatter(reduce_scatter(padded, "grp"), "dev")
    total = gather(gather(total, "dev"), "grp")
    order = cols * n_dev
    full = jnp.zeros((order, order), jnp.float32)
    for n, (a, b) in enumerate(lower_blocks(order // LANES)):
        block = total[n * LANES:(n + 1) * LANES]
        full = full.at[a * LANES:(a + 1) * LANES, b * LANES:(b + 1) * LANES].set(block)
    lower = lax.linalg.cholesky(full, symmetrize_input=False)
    return own_block(lower.T)


def solution(mesh):
    in_specs = (P(None, "dev", "grp", None), P())
    out_specs = P("dev", "grp")
    return jax.shard_map(
        per_device, mesh=mesh, in_specs=in_specs, out_specs=out_specs, check_vma=False
    )
```

```python
import functools

import jax
import jax.numpy as jnp
from jax import lax
from jax.experimental import pallas as pl
from jax.experimental.pallas import tpu as pltpu
from jax.sharding import PartitionSpec as P

LANES = 128


def project_kernel(rank, dest_ref, slab_ref, factor_ref, out_ref, wide_ref):
    cols, width, depth = slab_ref.shape
    half = width // 2
    flat = slab_ref[...].reshape(cols * width, depth)
    wide_ref[...] = jnp.dot(flat, factor_ref[...], preferred_element_type=jnp.float32)
    lane = lax.broadcasted_iota(jnp.int32, (cols, LANES), 1)
    for s in range(half):
        low = wide_ref[pl.ds(s, cols, stride=width), :]
        high = wide_ref[pl.ds(s + half, cols, stride=width), :]
        both = jnp.where(lane < rank, low, high)
        out_ref[:, s * LANES:(s + 1) * LANES] = both.astype(out_ref.dtype)


def project(slab, factor_pair, rank, dest, width):
    cols, total_width, depth = slab.shape
    block_cols = 16
    out_width = width * rank
    grid_spec = pltpu.PrefetchScalarGridSpec(
        num_scalar_prefetch=1,
        grid=(cols // block_cols,),
        in_specs=[
            pl.BlockSpec((block_cols, width, depth), lambda c, d: (c, d[0], 0)),
            pl.BlockSpec(factor_pair.shape, lambda c, d: (0, 0)),
        ],
        out_specs=pl.BlockSpec((block_cols, out_width), lambda c, d: (c, 0)),
        scratch_shapes=[pltpu.VMEM((block_cols * width, LANES), jnp.float32)],
    )
    return pl.pallas_call(
        functools.partial(project_kernel, rank),
        out_shape=jax.ShapeDtypeStruct((cols, out_width), jnp.bfloat16),
        grid_spec=grid_spec,
        compiler_params=pltpu.CompilerParams(vmem_limit_bytes=44 * 2**20),
        cost_estimate=pl.CostEstimate(
            flops=8 * cols * width * depth * rank,
            bytes_accessed=2 * cols * width * depth + 2 * cols * out_width,
            transcendentals=0,
        ),
        name="project",
    )(dest.reshape(1), slab, factor_pair)


def upper_blocks(count):
    return [(a, b) for a in range(count) for b in range(a, count)]


def gram_kernel(scale, count, place_ref, *refs):
    pieces = refs[:count]
    out_ref, full_ref = refs[count:]
    cols = pieces[0].shape[0]
    for i, piece in enumerate(pieces):
        start = pl.multiple_of(place_ref[i] * cols, 16)
        full_ref[pl.ds(start, cols), :] = piece[...]
    order = cols * count
    where = {ab: n for n, ab in enumerate(upper_blocks(order // LANES))}
    wide = 2 * LANES
    for tile in range(order // wide):
        left = full_ref[:(tile + 1) * wide, :]
        right = full_ref[tile * wide:(tile + 1) * wide, :]
        product = lax.dot_general(
            left, right, (((1,), (1,)), ((), ())), preferred_element_type=jnp.float32
        ) * scale
        for b in range(2 * tile, 2 * tile + 2):
            for a in range(b + 1):
                n = where[(a, b)]
                col = (b - 2 * tile) * LANES
                out_ref[n * LANES:(n + 1) * LANES, :] = product[a * LANES:(a + 1) * LANES, col:col + LANES]


def gram(pieces, places, scale):
    cols, width = pieces[0].shape
    count = len(pieces)
    order = cols * count
    rows = len(upper_blocks(order // LANES)) * LANES
    return pl.pallas_call(
        functools.partial(gram_kernel, scale, count),
        out_shape=jax.ShapeDtypeStruct((rows, LANES), jnp.float32),
        in_specs=[pl.BlockSpec(memory_space=pltpu.SMEM)]
        + [pl.BlockSpec(memory_space=pltpu.VMEM)] * count,
        out_specs=pl.BlockSpec(memory_space=pltpu.VMEM),
        scratch_shapes=[pltpu.VMEM((order, width), jnp.bfloat16)],
        compiler_params=pltpu.CompilerParams(vmem_limit_bytes=40 * 2**20),
        cost_estimate=pl.CostEstimate(
            flops=2 * order * order * width,
            bytes_accessed=2 * order * width + 4 * rows * LANES,
            transcendentals=0,
        ),
        name="gram",
    )(places, *pieces)


def reduce_scatter(x, axis):
    n = lax.axis_size(axis)
    shares = x.reshape(n, x.shape[0] // n, LANES)
    return lax.all_to_all(shares, axis, split_axis=0, concat_axis=0, tiled=True).sum(axis=0)


def gather(x, axis):
    n = lax.axis_size(axis)
    copies = jnp.broadcast_to(x[None], (n, *x.shape))
    return lax.all_to_all(copies, axis, split_axis=0, concat_axis=0, tiled=True).reshape(
        n * x.shape[0], LANES
    )


def spread_lane(rows, lane):
    return jnp.broadcast_to(rows[:, lane:lane + 1], rows.shape)


def spread_row(rows, row):
    return jnp.broadcast_to(rows[row:row + 1, :], rows.shape)


def factor_block(block, step):
    lane = lax.broadcasted_iota(jnp.int32, (step, LANES), 1)
    row = lax.broadcasted_iota(jnp.int32, (step, LANES), 0)
    rows = [block[i * step:(i + 1) * step, :] for i in range(LANES // step)]
    tri_rows, inv_rows = [], []
    for t, head in enumerate(rows):
        first = t * step
        inside = (lane >= first) & (lane < first + step)
        spread = [spread_lane(head, first + b) for b in range(step)]
        s = {(a, b): spread_row(spread[b], a) for a in range(step) for b in range(a, step)}
        r, inv_diag = {}, []
        for k in range(step):
            inv = lax.rsqrt(s[k, k])
            inv_diag.append(inv)
            for b in range(k, step):
                r[k, b] = s[k, b] * inv
            for a in range(k + 1, step):
                for b in range(a, step):
                    s[a, b] = s[a, b] - r[k, a] * r[k, b]
        tri, mix = [], []
        for k in range(step):
            raw = spread_row(head, k)
            x = raw
            y = jnp.where(inside, jnp.where(lane == first + k, 1.0, 0.0), raw)
            for m in range(k):
                x = x - r[m, k] * tri[m]
                y = y - r[m, k] * mix[m]
            tri.append(x * inv_diag[k])
            mix.append(y * inv_diag[k])
        tri_out, mix_out = tri[0], mix[0]
        for k in range(1, step):
            tri_out = jnp.where(row == k, tri[k], tri_out)
            mix_out = jnp.where(row == k, mix[k], mix_out)
        tri_rows.append(jnp.where(lane >= row + first, tri_out, 0.0))
        inv_rows.append(jnp.where(lane <= row + first, mix_out, 0.0))
        for i in range(t + 1, LANES // step):
            col, held = [], jnp.where(inside, 0.0, rows[i])
            for k in range(step):
                c = spread_lane(rows[i], first + k)
                for m in range(k):
                    c = c - r[m, k] * col[m]
                col.append(c * inv_diag[k])
                held = held - col[k] * mix[k]
            rows[i] = held
    return tri_rows, inv_rows


def triangle_kernel(count, place_ref, blocks_ref, out_ref, work_ref, tri_ref, inv_ref):
    step = 8
    high = lax.Precision.HIGHEST
    where = {ab: n for n, ab in enumerate(upper_blocks(count))}

    def at(a, b):
        return pl.ds(where[a, b] * LANES, LANES)

    work_ref[...] = blocks_ref[:len(where) * LANES, :]
    tri_ref[...] = jnp.zeros_like(tri_ref)
    for p in range(count):
        tri_rows, inv_rows = factor_block(work_ref[at(p, p), :], step)
        for i in range(LANES // step):
            tri_ref[p * LANES + i * step:p * LANES + (i + 1) * step, p * LANES:(p + 1) * LANES] = tri_rows[i]
            inv_ref[i * step:(i + 1) * step, :] = inv_rows[i]
        for q in range(p + 1, count):
            tri_ref[p * LANES:(p + 1) * LANES, q * LANES:(q + 1) * LANES] = jnp.dot(
                inv_ref[...], work_ref[at(p, q), :], precision=high, preferred_element_type=jnp.float32
            )
        for a in range(p + 1, count):
            for b in range(a, count):
                work_ref[at(a, b), :] -= lax.dot_general(
                    tri_ref[p * LANES:(p + 1) * LANES, a * LANES:(a + 1) * LANES],
                    tri_ref[p * LANES:(p + 1) * LANES, b * LANES:(b + 1) * LANES],
                    (((0,), (0,)), ((), ())), precision=high, preferred_element_type=jnp.float32,
                )
    out_rows = out_ref.shape[0]
    row = pl.multiple_of(place_ref[0] * out_rows, 8)
    col = pl.multiple_of(place_ref[1] * LANES, LANES)
    out_ref[...] = tri_ref[pl.ds(row, out_rows), pl.ds(col, LANES)]


def own_triangle(blocks, order):
    row_count = order // lax.axis_size("dev")
    col_count = order // lax.axis_size("grp")
    grp = lax.axis_index("grp")
    place = jnp.stack([lax.axis_index("dev"), grp * col_count // LANES]).astype(jnp.int32)
    count = order // LANES
    rows = len(upper_blocks(count)) * LANES
    out = pl.pallas_call(
        functools.partial(triangle_kernel, count),
        out_shape=jax.ShapeDtypeStruct((row_count, LANES), jnp.float32),
        in_specs=[pl.BlockSpec(memory_space=pltpu.SMEM), pl.BlockSpec(memory_space=pltpu.VMEM)],
        out_specs=pl.BlockSpec(memory_space=pltpu.VMEM),
        scratch_shapes=[
            pltpu.VMEM((rows, LANES), jnp.float32),
            pltpu.VMEM((order, order), jnp.float32),
            pltpu.VMEM((LANES, LANES), jnp.float32),
        ],
        compiler_params=pltpu.CompilerParams(vmem_limit_bytes=32 * 2**20),
        cost_estimate=pl.CostEstimate(
            flops=order**3, bytes_accessed=4 * order * order, transcendentals=order
        ),
        name="triangle",
    )(place, blocks)
    if col_count == LANES:
        return out
    return lax.dynamic_slice(out, (0, grp * col_count % LANES), (row_count, col_count))


def per_device(tensor_slab, mode_factor):
    depth, cols, slab_depth, species = tensor_slab.shape
    rank = mode_factor.shape[1]
    n_dev = lax.axis_size("dev")
    n_grp = lax.axis_size("grp")
    me = lax.axis_index("dev")
    slab = tensor_slab.transpose(1, 2, 3, 0).reshape(cols, slab_depth * species, depth)
    width = slab_depth * species // n_dev
    factor_pair = jnp.concatenate([mode_factor, mode_factor], axis=1)
    pieces, places = [], []
    half = n_dev // 2
    near, far = list(range(1, half)), list(range(half, n_dev))
    order = far[:1] + near[:1] + far[1:2] + near[1:2] + far[2:] + near[2:] + [0]
    for offset in order:
        other = jnp.bitwise_xor(me, offset).astype(jnp.int32)
        piece = project(slab, factor_pair, rank, other, width)
        if offset:
            piece = lax.ppermute(piece, "dev", [(i, i ^ offset) for i in range(n_dev)])
        pieces.append(piece)
        places.append(other)
    row_total = rank * slab_depth * species * n_grp
    part = gram(pieces, jnp.stack(places), 1.0 / row_total)
    rows = part.shape[0]
    unit = 8 * n_dev * n_grp
    padded = jnp.pad(part, ((0, -rows % unit), (0, 0)))
    total = reduce_scatter(reduce_scatter(padded, "grp"), "dev")
    total = gather(gather(total, "dev"), "grp")
    return own_triangle(total, cols * n_dev)


def solution(mesh):
    in_specs = (P(None, "dev", "grp", None), P())
    out_specs = P("dev", "grp")
    return jax.shard_map(
        per_device, mesh=mesh, in_specs=in_specs, out_specs=out_specs, check_vma=False
    )
```

```python
import functools

import jax
import jax.numpy as jnp
from jax import lax
from jax.experimental import pallas as pl
from jax.experimental.pallas import tpu as pltpu
from jax.sharding import PartitionSpec as P

LANES = 128


def project_kernel(rank, slabs, *refs):
    slab_refs = refs[slabs:2 * slabs]
    factor_ref = refs[2 * slabs]
    out_refs = refs[2 * slabs + 1:-1]
    wide_ref = refs[-1]
    cols, width, depth = slab_refs[0].shape
    half = width // 2
    pitch = width + 1
    lane = lax.broadcasted_iota(jnp.int32, (cols, LANES), 1)
    for i, slab_ref in enumerate(slab_refs):
        flat = slab_ref[...].reshape(cols * width, depth)
        wide = jnp.dot(flat, factor_ref[...], preferred_element_type=jnp.float32)
        base = i * cols * pitch
        for c in range(cols):
            wide_ref[base + c * pitch:base + c * pitch + width, :] = wide[c * width:(c + 1) * width, :]
        for s in range(half):
            low = wide_ref[pl.ds(base + s, cols, stride=pitch), :]
            high = wide_ref[pl.ds(base + s + half, cols, stride=pitch), :]
            both = jnp.where(lane < rank, low, high).astype(jnp.bfloat16)
            at = (i * half + s) * LANES
            out_refs[0][:, at:at + LANES] = both
            if i:
                out_refs[i][:, s * LANES:(s + 1) * LANES] = both


def project(slab, factor_pair, rank, dests, width):
    cols, total_width, depth = slab.shape
    block_cols = 16
    out_width = width * rank
    slabs = len(dests)
    widths = [slabs * out_width] + [out_width] * (slabs - 1)
    grid_spec = pltpu.PrefetchScalarGridSpec(
        num_scalar_prefetch=slabs,
        grid=(cols // block_cols,),
        in_specs=[
            pl.BlockSpec((block_cols, width, depth), lambda c, *d, i=i: (c, d[i][0], 0))
            for i in range(slabs)
        ]
        + [pl.BlockSpec(factor_pair.shape, lambda c, *d: (0, 0))],
        out_specs=[pl.BlockSpec((block_cols, w), lambda c, *d: (c, 0)) for w in widths],
        scratch_shapes=[pltpu.VMEM((slabs * block_cols * (width + 1) + 7, LANES), jnp.float32)],
    )
    return pl.pallas_call(
        functools.partial(project_kernel, rank, slabs),
        out_shape=[jax.ShapeDtypeStruct((cols, w), jnp.bfloat16) for w in widths],
        grid_spec=grid_spec,
        compiler_params=pltpu.CompilerParams(vmem_limit_bytes=44 * 2**20),
        cost_estimate=pl.CostEstimate(
            flops=8 * slabs * cols * width * depth * rank,
            bytes_accessed=2 * slabs * cols * width * depth + 2 * cols * sum(widths),
            transcendentals=0,
        ),
        name="project",
    )(*[d.reshape(1) for d in dests], *[slab] * slabs, factor_pair)


def upper_blocks(count):
    return [(a, b) for a in range(count) for b in range(a, count)]


def gram_near_kernel(scale, width, count, place_ref, *refs):
    pieces = refs[:count]
    out_ref, full_ref = refs[count:]
    cols = pieces[0].shape[0]
    for i, piece in enumerate(pieces):
        start = pl.multiple_of(place_ref[i] * cols, 16)
        first = 0 if i != 1 else width
        full_ref[pl.ds(start, cols), first:first + piece.shape[1]] = piece[...]
    order = full_ref.shape[0]
    product = lax.dot_general(
        full_ref[...], full_ref[...], (((1,), (1,)), ((), ())), preferred_element_type=jnp.float32
    ) * scale
    for n, (a, b) in enumerate(upper_blocks(order // LANES)):
        out_ref[n * LANES:(n + 1) * LANES, :] = product[a * LANES:(a + 1) * LANES, b * LANES:(b + 1) * LANES]


def gram_cross_kernel(scale, width, count, place_ref, *refs):
    pieces = refs[:count]
    out_ref, full_ref = refs[count:]
    cols = pieces[0].shape[0]
    for i, piece in enumerate(pieces):
        start = pl.multiple_of(place_ref[i] * cols, 16)
        full_ref[pl.ds(start, cols), :] = piece[:, :width]
    half = full_ref.shape[0] // 2
    product = lax.dot_general(
        full_ref[:half, :], full_ref[half:, :], (((1,), (1,)), ((), ())), preferred_element_type=jnp.float32
    ) * scale
    blocks = half // LANES
    for a in range(blocks):
        for b in range(blocks):
            n = a * blocks + b
            out_ref[n * LANES:(n + 1) * LANES, :] = product[a * LANES:(a + 1) * LANES, b * LANES:(b + 1) * LANES]


def gram(kernel, pieces, places, scale, width, scratch, blocks, name):
    rows = blocks * LANES
    return pl.pallas_call(
        functools.partial(kernel, scale, width, len(pieces)),
        out_shape=jax.ShapeDtypeStruct((rows, LANES), jnp.float32),
        in_specs=[pl.BlockSpec(memory_space=pltpu.SMEM)]
        + [pl.BlockSpec(memory_space=pltpu.VMEM)] * len(pieces),
        out_specs=pl.BlockSpec(memory_space=pltpu.VMEM),
        scratch_shapes=[pltpu.VMEM(scratch, jnp.bfloat16)],
        compiler_params=pltpu.CompilerParams(vmem_limit_bytes=40 * 2**20),
        cost_estimate=pl.CostEstimate(
            flops=2 * scratch[0] * scratch[0] * scratch[1],
            bytes_accessed=2 * scratch[0] * scratch[1] + 4 * rows * LANES,
            transcendentals=0,
        ),
        name=name,
    )(places, *pieces)


BOTH = ("grp", "dev")


def exchange(x):
    return lax.all_to_all(x, BOTH, split_axis=0, concat_axis=0, tiled=True)


def shares(x, devices):
    rows = x.shape[0]
    x = jnp.pad(x, ((0, -rows % (8 * devices)), (0, 0)))
    return x.reshape(devices, x.shape[0] // devices, LANES)


def gather(x, devices):
    return exchange(jnp.broadcast_to(x[None], (devices, *x.shape)))


def spread_lane(rows, lane):
    return jnp.broadcast_to(rows[:, lane:lane + 1], rows.shape)


def spread_row(rows, row):
    return jnp.broadcast_to(rows[row:row + 1, :], rows.shape)


def factor_block(block, step):
    lane = lax.broadcasted_iota(jnp.int32, (step, LANES), 1)
    row = lax.broadcasted_iota(jnp.int32, (step, LANES), 0)
    rows = [block[i * step:(i + 1) * step, :] for i in range(LANES // step)]
    tri_rows, inv_rows = [], []
    for t, head in enumerate(rows):
        first = t * step
        inside = (lane >= first) & (lane < first + step)
        spread = [spread_lane(head, first + b) for b in range(step)]
        s = {(a, b): spread_row(spread[b], a) for a in range(step) for b in range(a, step)}
        r, inv_diag = {}, []
        for k in range(step):
            inv = lax.rsqrt(s[k, k])
            inv_diag.append(inv)
            for b in range(k, step):
                r[k, b] = s[k, b] * inv
            for a in range(k + 1, step):
                for b in range(a, step):
                    s[a, b] = s[a, b] - r[k, a] * r[k, b]
        tri, mix = [], []
        for k in range(step):
            raw = spread_row(head, k)
            x = raw
            y = jnp.where(inside, jnp.where(lane == first + k, 1.0, 0.0), raw)
            for m in range(k):
                x = x - r[m, k] * tri[m]
                y = y - r[m, k] * mix[m]
            tri.append(x * inv_diag[k])
            mix.append(y * inv_diag[k])
        tri_out, mix_out = tri[0], mix[0]
        for k in range(1, step):
            tri_out = jnp.where(row == k, tri[k], tri_out)
            mix_out = jnp.where(row == k, mix[k], mix_out)
        tri_rows.append(jnp.where(lane >= row + first, tri_out, 0.0))
        inv_rows.append(jnp.where(lane <= row + first, mix_out, 0.0))
        for i in range(t + 1, LANES // step):
            col, held = [], jnp.where(inside, 0.0, rows[i])
            for k in range(step):
                c = spread_lane(rows[i], first + k)
                for m in range(k):
                    c = c - r[m, k] * col[m]
                col.append(c * inv_diag[k])
                held = held - col[k] * mix[k]
            rows[i] = held
    return tri_rows, inv_rows


HIGH = lax.Precision.HIGHEST


def block_at(ref, a, b):
    return ref.at[a * LANES:(a + 1) * LANES, b * LANES:(b + 1) * LANES]


def factor_into(tri_ref, inv_ref, work_ref, p):
    step = 8
    tri_rows, inv_rows = factor_block(block_at(work_ref, p, p)[...], step)
    for i in range(LANES // step):
        at = slice(p * LANES + i * step, p * LANES + (i + 1) * step)
        tri_ref[at, p * LANES:(p + 1) * LANES] = tri_rows[i]
        inv_ref[at, :] = inv_rows[i]


def solve_row(tri_ref, inv_ref, work_ref, p, q):
    block_at(tri_ref, p, q)[...] = jnp.dot(
        inv_ref[p * LANES:(p + 1) * LANES, :], block_at(work_ref, p, q)[...],
        precision=HIGH, preferred_element_type=jnp.float32,
    )


def take_off(tri_ref, work_ref, p, a, b):
    block_at(work_ref, a, b)[...] -= lax.dot_general(
        block_at(tri_ref, p, a)[...], block_at(tri_ref, p, b)[...],
        (((0,), (0,)), ((), ())), precision=HIGH, preferred_element_type=jnp.float32,
    )


def first_triangle_kernel(count, blocks_ref, tri_ref, inv_ref, work_ref):
    for n, (a, b) in enumerate(upper_blocks(count)):
        block_at(work_ref, a, b)[...] = blocks_ref[n * LANES:(n + 1) * LANES, :]
    tri_ref[...] = jnp.zeros_like(tri_ref)
    for p in range(count):
        factor_into(tri_ref, inv_ref, work_ref, p)
        for q in range(p + 1, count):
            solve_row(tri_ref, inv_ref, work_ref, p, q)
        for a, b in upper_blocks(count):
            if a > p:
                take_off(tri_ref, work_ref, p, a, b)


def first_triangle(blocks, count):
    size = count * LANES
    return pl.pallas_call(
        functools.partial(first_triangle_kernel, count),
        out_shape=[
            jax.ShapeDtypeStruct((size, size), jnp.float32),
            jax.ShapeDtypeStruct((size, LANES), jnp.float32),
        ],
        in_specs=[pl.BlockSpec(memory_space=pltpu.VMEM)],
        out_specs=[pl.BlockSpec(memory_space=pltpu.VMEM)] * 2,
        scratch_shapes=[pltpu.VMEM((size, size), jnp.float32)],
        compiler_params=pltpu.CompilerParams(vmem_limit_bytes=32 * 2**20),
        cost_estimate=pl.CostEstimate(
            flops=size**3, bytes_accessed=8 * size * size, transcendentals=size
        ),
        name="first_triangle",
    )(blocks)


def last_triangle_kernel(count, place_ref, done_ref, done_inv_ref, cross_ref, last_ref, out_ref, work_ref, tri_ref, inv_ref):
    half = count // 2
    size = half * LANES
    for a in range(half):
        for b in range(half):
            n = a * half + b
            block_at(work_ref, a, half + b)[...] = cross_ref[n * LANES:(n + 1) * LANES, :]
    for n, (a, b) in enumerate(upper_blocks(half)):
        block_at(work_ref, half + a, half + b)[...] = last_ref[n * LANES:(n + 1) * LANES, :]
    tri_ref[...] = jnp.zeros_like(tri_ref)
    tri_ref[:size, :size] = done_ref[...]
    inv_ref[:size, :] = done_inv_ref[...]
    for p in range(count):
        if p >= half:
            factor_into(tri_ref, inv_ref, work_ref, p)
        for q in range(max(p + 1, half), count):
            solve_row(tri_ref, inv_ref, work_ref, p, q)
        for a, b in upper_blocks(count):
            if a > p and b >= half:
                take_off(tri_ref, work_ref, p, a, b)
    out_rows = out_ref.shape[0]
    row = pl.multiple_of(place_ref[0] * out_rows, 8)
    col = pl.multiple_of(place_ref[1] * LANES, LANES)
    out_ref[...] = tri_ref[pl.ds(row, out_rows), pl.ds(col, LANES)]


def last_triangle(done, done_inv, cross, last, order):
    row_count = order // lax.axis_size("dev")
    col_count = order // lax.axis_size("grp")
    grp = lax.axis_index("grp")
    place = jnp.stack([lax.axis_index("dev"), grp * col_count // LANES]).astype(jnp.int32)
    out = pl.pallas_call(
        functools.partial(last_triangle_kernel, order // LANES),
        out_shape=jax.ShapeDtypeStruct((row_count, LANES), jnp.float32),
        in_specs=[pl.BlockSpec(memory_space=pltpu.SMEM)] + [pl.BlockSpec(memory_space=pltpu.VMEM)] * 4,
        out_specs=pl.BlockSpec(memory_space=pltpu.VMEM),
        scratch_shapes=[
            pltpu.VMEM((order, order), jnp.float32),
            pltpu.VMEM((order, order), jnp.float32),
            pltpu.VMEM((order, LANES), jnp.float32),
        ],
        compiler_params=pltpu.CompilerParams(vmem_limit_bytes=32 * 2**20),
        cost_estimate=pl.CostEstimate(
            flops=order**3, bytes_accessed=4 * order * order, transcendentals=order
        ),
        name="last_triangle",
    )(place, done, done_inv, cross, last)
    if col_count == LANES:
        return out
    return lax.dynamic_slice(out, (0, grp * col_count % LANES), (row_count, col_count))


def per_device(tensor_slab, mode_factor):
    depth, cols, slab_depth, species = tensor_slab.shape
    rank = mode_factor.shape[1]
    n_dev = lax.axis_size("dev")
    n_grp = lax.axis_size("grp")
    devices = n_dev * n_grp
    me = lax.axis_index("dev").astype(jnp.int32)
    slab = tensor_slab.transpose(1, 2, 3, 0).reshape(cols, slab_depth * species, depth)
    width = slab_depth * species // n_dev
    out_width = width * rank
    factor_pair = jnp.concatenate([mode_factor, mode_factor], axis=1)
    scale = 1.0 / (rank * slab_depth * species * n_grp)
    half = n_dev // 2
    order = cols * n_dev

    def partner(offset):
        return jnp.bitwise_xor(me, offset)

    def send(piece, offset):
        return lax.ppermute(piece, "dev", [(i, i ^ offset) for i in range(n_dev)])

    [mirror] = project(slab, factor_pair, rank, [partner(half)], width)
    far = [send(mirror, half)]
    near = []
    for offset in range(1, half):
        dests = [partner(offset), partner(offset + half)]
        if offset == 1:
            mirror, *dests = lax.optimization_barrier((mirror, *dests))
        elif offset == half - 1:
            far[0], *dests = lax.optimization_barrier((far[0], *dests))
        both, other = project(slab, factor_pair, rank, dests, width)
        near.append(send(both, offset))
        far.append(send(other, offset + half))
    [own] = project(slab, factor_pair, rank, [me], width)

    near_places = jnp.stack([me % half, me % half] + [partner(o) % half for o in range(1, half)])
    part = gram(
        gram_near_kernel, [own, mirror, *near], near_places, scale, out_width,
        (order // 2, 2 * out_width), len(upper_blocks(order // 2 // LANES)), "gram_near",
    )
    parts = exchange(shares(part, devices))
    parts = parts.reshape(n_grp, 2, half, *parts.shape[1:]).sum(axis=(0, 2))
    halves = gather(parts, devices)
    halves = halves.transpose(1, 0, 2, 3).reshape(2, -1, LANES)
    done, done_inv = first_triangle(halves[0], order // 2 // LANES)

    places = jnp.stack([partner(o) for o in [*range(half, n_dev), 0, *range(1, half)]])
    own, done = lax.optimization_barrier((own, done))
    cross = gram(
        gram_cross_kernel, [*far, own, *near], places, scale, out_width,
        (order, out_width), (order // 2 // LANES) ** 2, "gram_cross",
    )
    cross = exchange(shares(cross, devices)).sum(axis=0)
    cross = gather(cross, devices).reshape(-1, LANES)
    return last_triangle(done, done_inv, cross, halves[1], order)


def solution(mesh):
    in_specs = (P(None, "dev", "grp", None), P())
    out_specs = P("dev", "grp")
    return jax.shard_map(
        per_device, mesh=mesh, in_specs=in_specs, out_specs=out_specs, check_vma=False
    )
```

```python
import functools

import jax
import jax.numpy as jnp
from jax import lax
from jax.experimental import pallas as pl
from jax.experimental.pallas import tpu as pltpu
from jax.sharding import PartitionSpec as P

LANES = 128
GROUP = ("pair", "core")


def project_kernel(dest_ref, slab_ref, factor_ref, out_ref, wide_ref):
    cols, width, depth = slab_ref.shape
    rank = factor_ref.shape[0]
    half = width // 2
    pitch = width + 1
    lane = lax.broadcasted_iota(jnp.int32, (cols, LANES), 1)
    flat = slab_ref[...].reshape(cols * width, depth)
    twice = jnp.concatenate([factor_ref[...], factor_ref[...]], axis=0)
    wide = lax.dot_general(
        flat, twice, (((1,), (1,)), ((), ())), preferred_element_type=jnp.float32
    )
    for c in range(cols):
        wide_ref[c * pitch:c * pitch + width, :] = wide[c * width:(c + 1) * width, :]
    for s in range(half):
        low = wide_ref[pl.ds(s, cols, stride=pitch), :]
        high = wide_ref[pl.ds(s + half, cols, stride=pitch), :]
        both = jnp.where(lane < rank, low, high)
        out_ref[:, s * LANES:(s + 1) * LANES] = both.astype(out_ref.dtype)


def project(slab, factor, dest, width):
    cols, total_width, depth = slab.shape
    rank = factor.shape[0]
    block_cols = 16
    out_width = width * rank
    grid_spec = pltpu.PrefetchScalarGridSpec(
        num_scalar_prefetch=1,
        grid=(cols // block_cols,),
        in_specs=[
            pl.BlockSpec((block_cols, width, depth), lambda c, d: (c, d[0], 0)),
            pl.BlockSpec(factor.shape, lambda c, d: (0, 0)),
        ],
        out_specs=pl.BlockSpec((block_cols, out_width), lambda c, d: (c, 0)),
        scratch_shapes=[pltpu.VMEM((block_cols * (width + 1) + 8, LANES), jnp.float32)],
    )
    return pl.pallas_call(
        project_kernel,
        out_shape=jax.ShapeDtypeStruct((cols, out_width), jnp.bfloat16),
        grid_spec=grid_spec,
        compiler_params=pltpu.CompilerParams(vmem_limit_bytes=44 * 2**20),
        cost_estimate=pl.CostEstimate(
            flops=8 * cols * width * depth * rank,
            bytes_accessed=2 * cols * width * depth + 2 * cols * out_width,
            transcendentals=0,
        ),
        name="project",
    )(dest.reshape(1), slab, factor)


def upper_blocks(count):
    return [(a, b) for a in range(count) for b in range(a, count)]


def gram_kernel(scale, count, place_ref, *refs):
    pieces = refs[:count]
    out_ref, full_ref = refs[count:]
    cols = pieces[0].shape[0]
    for i, piece in enumerate(pieces):
        start = pl.multiple_of(place_ref[i] * cols, 16)
        full_ref[pl.ds(start, cols), :] = piece[...]
    order = cols * count
    where = {ab: n for n, ab in enumerate(upper_blocks(order // LANES))}
    wide = 2 * LANES
    for tile in range(order // wide):
        left = full_ref[:(tile + 1) * wide, :]
        right = full_ref[tile * wide:(tile + 1) * wide, :]
        product = lax.dot_general(
            left, right, (((1,), (1,)), ((), ())), preferred_element_type=jnp.float32
        ) * scale
        for b in range(2 * tile, 2 * tile + 2):
            for a in range(b + 1):
                n = where[(a, b)]
                col = (b - 2 * tile) * LANES
                out_ref[n * LANES:(n + 1) * LANES, :] = product[a * LANES:(a + 1) * LANES, col:col + LANES]


def gram(pieces, places, scale):
    cols, width = pieces[0].shape
    count = len(pieces)
    order = cols * count
    rows = len(upper_blocks(order // LANES)) * LANES
    return pl.pallas_call(
        functools.partial(gram_kernel, scale, count),
        out_shape=jax.ShapeDtypeStruct((rows, LANES), jnp.float32),
        in_specs=[pl.BlockSpec(memory_space=pltpu.SMEM)]
        + [pl.BlockSpec(memory_space=pltpu.VMEM)] * count,
        out_specs=pl.BlockSpec(memory_space=pltpu.VMEM),
        scratch_shapes=[pltpu.VMEM((order, width), jnp.bfloat16)],
        compiler_params=pltpu.CompilerParams(vmem_limit_bytes=40 * 2**20),
        cost_estimate=pl.CostEstimate(
            flops=2 * order * order * width,
            bytes_accessed=2 * order * width + 4 * rows * LANES,
            transcendentals=0,
        ),
        name="gram",
    )(places, *pieces)


CHIPS = ("pair", "dev")


def exchange(x):
    return lax.all_to_all(x, CHIPS, split_axis=0, concat_axis=0, tiled=True)


def swap_cores(x):
    return lax.ppermute(x, "core", [(0, 1), (1, 0)])


def summed_halves(part):
    chips = lax.axis_size(CHIPS)
    core = lax.axis_index("core")
    rows = part.shape[0]
    part = jnp.pad(part, ((0, -rows % (16 * chips)), (0, 0)))
    half = part.shape[0] // 2
    theirs = lax.dynamic_slice_in_dim(part, (1 - core) * half, half)
    mine = lax.dynamic_slice_in_dim(part, core * half, half)
    mine = mine + swap_cores(theirs)
    share = exchange(mine.reshape(chips, half // chips, LANES)).sum(axis=0)
    mine = exchange(jnp.broadcast_to(share[None], (chips, *share.shape))).reshape(half, LANES)
    return mine, swap_cores(mine)


def spread_lane(rows, lane):
    return jnp.broadcast_to(rows[:, lane:lane + 1], rows.shape)


def spread_row(rows, row):
    return jnp.broadcast_to(rows[row:row + 1, :], rows.shape)


def factor_block(block, step):
    lane = lax.broadcasted_iota(jnp.int32, (step, LANES), 1)
    row = lax.broadcasted_iota(jnp.int32, (step, LANES), 0)
    rows = [block[i * step:(i + 1) * step, :] for i in range(LANES // step)]
    tri_rows, inv_rows = [], []
    for t, head in enumerate(rows):
        first = t * step
        inside = (lane >= first) & (lane < first + step)
        spread = [spread_lane(head, first + b) for b in range(step)]
        s = {(a, b): spread_row(spread[b], a) for a in range(step) for b in range(a, step)}
        r, inv_diag = {}, []
        for k in range(step):
            inv = lax.rsqrt(s[k, k])
            inv_diag.append(inv)
            for b in range(k, step):
                r[k, b] = s[k, b] * inv
            for a in range(k + 1, step):
                for b in range(a, step):
                    s[a, b] = s[a, b] - r[k, a] * r[k, b]
        tri, mix = [], []
        for k in range(step):
            raw = spread_row(head, k)
            x = raw
            y = jnp.where(inside, jnp.where(lane == first + k, 1.0, 0.0), raw)
            for m in range(k):
                x = x - r[m, k] * tri[m]
                y = y - r[m, k] * mix[m]
            tri.append(x * inv_diag[k])
            mix.append(y * inv_diag[k])
        tri_out, mix_out = tri[0], mix[0]
        for k in range(1, step):
            tri_out = jnp.where(row == k, tri[k], tri_out)
            mix_out = jnp.where(row == k, mix[k], mix_out)
        tri_rows.append(jnp.where(lane >= row + first, tri_out, 0.0))
        inv_rows.append(jnp.where(lane <= row + first, mix_out, 0.0))
        for i in range(t + 1, LANES // step):
            col, held = [], jnp.where(inside, 0.0, rows[i])
            for k in range(step):
                c = spread_lane(rows[i], first + k)
                for m in range(k):
                    c = c - r[m, k] * col[m]
                col.append(c * inv_diag[k])
                held = held - col[k] * mix[k]
            rows[i] = held
    return tri_rows, inv_rows


def triangle_kernel(count, place_ref, mine_ref, other_ref, out_ref, work_ref, tri_ref, inv_ref):
    step = 8
    high = lax.Precision.HIGHEST
    where = {ab: n for n, ab in enumerate(upper_blocks(count))}

    def at(a, b):
        return pl.ds(where[a, b] * LANES, LANES)

    half = mine_ref.shape[0]
    first_core = place_ref[2] == 0
    work_ref[:half, :] = jnp.where(first_core, mine_ref[...], other_ref[...])
    left = len(where) * LANES - half
    work_ref[half:, :] = jnp.where(first_core, other_ref[:left, :], mine_ref[:left, :])
    tri_ref[...] = jnp.zeros_like(tri_ref)
    for p in range(count):
        tri_rows, inv_rows = factor_block(work_ref[at(p, p), :], step)
        for i in range(LANES // step):
            tri_ref[p * LANES + i * step:p * LANES + (i + 1) * step, p * LANES:(p + 1) * LANES] = tri_rows[i]
            inv_ref[i * step:(i + 1) * step, :] = inv_rows[i]
        for q in range(p + 1, count):
            tri_ref[p * LANES:(p + 1) * LANES, q * LANES:(q + 1) * LANES] = jnp.dot(
                inv_ref[...], work_ref[at(p, q), :], precision=high, preferred_element_type=jnp.float32
            )
        for a in range(p + 1, count):
            for b in range(a, count):
                work_ref[at(a, b), :] -= lax.dot_general(
                    tri_ref[p * LANES:(p + 1) * LANES, a * LANES:(a + 1) * LANES],
                    tri_ref[p * LANES:(p + 1) * LANES, b * LANES:(b + 1) * LANES],
                    (((0,), (0,)), ((), ())), precision=high, preferred_element_type=jnp.float32,
                )
    out_rows = out_ref.shape[0]
    row = pl.multiple_of(place_ref[0] * out_rows, 8)
    col = pl.multiple_of(place_ref[1] * LANES, LANES)
    out_ref[...] = tri_ref[pl.ds(row, out_rows), pl.ds(col, LANES)]


def own_triangle(mine, other, order):
    row_count = order // lax.axis_size("dev")
    col_count = order // lax.axis_size(GROUP)
    grp = lax.axis_index(GROUP)
    place = [lax.axis_index("dev"), grp * col_count // LANES, lax.axis_index("core")]
    place = jnp.stack(place).astype(jnp.int32)
    count = order // LANES
    rows = len(upper_blocks(count)) * LANES
    out = pl.pallas_call(
        functools.partial(triangle_kernel, count),
        out_shape=jax.ShapeDtypeStruct((row_count, LANES), jnp.float32),
        in_specs=[pl.BlockSpec(memory_space=pltpu.SMEM)] + [pl.BlockSpec(memory_space=pltpu.VMEM)] * 2,
        out_specs=pl.BlockSpec(memory_space=pltpu.VMEM),
        scratch_shapes=[
            pltpu.VMEM((rows, LANES), jnp.float32),
            pltpu.VMEM((order, order), jnp.float32),
            pltpu.VMEM((LANES, LANES), jnp.float32),
        ],
        compiler_params=pltpu.CompilerParams(vmem_limit_bytes=32 * 2**20),
        cost_estimate=pl.CostEstimate(
            flops=order**3, bytes_accessed=4 * order * order, transcendentals=order
        ),
        name="triangle",
    )(place, mine, other)
    if col_count == LANES:
        return out
    return lax.dynamic_slice(out, (0, grp * col_count % LANES), (row_count, col_count))


def per_device(tensor_slab, mode_factor):
    depth, cols, slab_depth, species = tensor_slab.shape
    rank = mode_factor.shape[1]
    n_dev = lax.axis_size("dev")
    n_grp = lax.axis_size(GROUP)
    me = lax.axis_index("dev")
    slab = tensor_slab.transpose(1, 2, 3, 0).reshape(cols, slab_depth * species, depth)
    width = slab_depth * species // n_dev
    factor = mode_factor.T
    pieces, places = [], []
    half = n_dev // 2
    near, far = list(range(1, half)), list(range(half, n_dev))
    order = far[:1] + near[:1] + far[1:2] + near[1:2] + far[2:] + near[2:] + [0]
    for offset in order:
        other = jnp.bitwise_xor(me, offset).astype(jnp.int32)
        piece = project(slab, factor, other, width)
        if offset:
            piece = lax.ppermute(piece, "dev", [(i, i ^ offset) for i in range(n_dev)])
        pieces.append(piece)
        places.append(other)
    row_total = rank * slab_depth * species * n_grp
    part = gram(pieces, jnp.stack(places), 1.0 / row_total)
    mine, other = summed_halves(part)
    return own_triangle(mine, other, cols * n_dev)


def solution(mesh):
    cores = 2
    devices = mesh.devices
    split = jax.sharding.Mesh(
        devices.reshape(devices.shape[0] // cores, cores, devices.shape[1]), (*GROUP, "dev")
    )
    in_specs = (P(None, "dev", GROUP, None), P())
    out_specs = P("dev", GROUP)
    return jax.shard_map(
        per_device, mesh=split, in_specs=in_specs, out_specs=out_specs, check_vma=False
    )
```

```python
import functools

import jax
import jax.numpy as jnp
from jax import lax
from jax.experimental import pallas as pl
from jax.experimental.pallas import tpu as pltpu
from jax.sharding import PartitionSpec as P

LANES = 128
GROUP = ("pair", "core")


def project_kernel(dest_ref, slab_ref, factor_ref, out_ref, wide_ref):
    cols, width, depth = slab_ref.shape
    rank = factor_ref.shape[0]
    half = width // 2
    pitch = width + 1
    lane = lax.broadcasted_iota(jnp.int32, (cols, LANES), 1)
    flat = slab_ref[...].reshape(cols * width, depth)
    twice = jnp.concatenate([factor_ref[...], factor_ref[...]], axis=0)
    wide = lax.dot_general(
        flat, twice, (((1,), (1,)), ((), ())), preferred_element_type=jnp.float32
    )
    for c in range(cols):
        wide_ref[c * pitch:c * pitch + width, :] = wide[c * width:(c + 1) * width, :]
    for s in range(half):
        low = wide_ref[pl.ds(s, cols, stride=pitch), :]
        high = wide_ref[pl.ds(s + half, cols, stride=pitch), :]
        both = jnp.where(lane < rank, low, high)
        out_ref[:, s * LANES:(s + 1) * LANES] = both.astype(out_ref.dtype)


def project(slab, factor, dest, width, first, cols):
    depth = slab.shape[2]
    rank = factor.shape[0]
    block_cols = 16
    first_block = first // block_cols
    out_width = width * rank
    grid_spec = pltpu.PrefetchScalarGridSpec(
        num_scalar_prefetch=1,
        grid=(cols // block_cols,),
        in_specs=[
            pl.BlockSpec((block_cols, width, depth), lambda c, d: (first_block + c, d[0], 0)),
            pl.BlockSpec(factor.shape, lambda c, d: (0, 0)),
        ],
        out_specs=pl.BlockSpec((block_cols, out_width), lambda c, d: (c, 0)),
        scratch_shapes=[pltpu.VMEM((block_cols * (width + 1) + 8, LANES), jnp.float32)],
    )
    return pl.pallas_call(
        project_kernel,
        out_shape=jax.ShapeDtypeStruct((cols, out_width), jnp.bfloat16),
        grid_spec=grid_spec,
        compiler_params=pltpu.CompilerParams(vmem_limit_bytes=44 * 2**20),
        cost_estimate=pl.CostEstimate(
            flops=8 * cols * width * depth * rank,
            bytes_accessed=2 * cols * width * depth + 2 * cols * out_width,
            transcendentals=0,
        ),
        name="project",
    )(dest.reshape(1), slab, factor)


def upper_blocks(count):
    return [(a, b) for a in range(count) for b in range(a, count)]


def gram_kernel(scale, count, place_ref, *refs):
    pieces = refs[:count]
    out_ref, full_ref = refs[count:]
    for i, piece in enumerate(pieces):
        start = pl.multiple_of(place_ref[i], 16)
        full_ref[pl.ds(start, piece.shape[0]), :] = piece[...]
    order = full_ref.shape[0]
    where = {ab: n for n, ab in enumerate(upper_blocks(order // LANES))}
    wide = 2 * LANES
    for tile in range(order // wide):
        left = full_ref[:(tile + 1) * wide, :]
        right = full_ref[tile * wide:(tile + 1) * wide, :]
        product = lax.dot_general(
            left, right, (((1,), (1,)), ((), ())), preferred_element_type=jnp.float32
        ) * scale
        for b in range(2 * tile, 2 * tile + 2):
            for a in range(b + 1):
                n = where[(a, b)]
                col = (b - 2 * tile) * LANES
                out_ref[n * LANES:(n + 1) * LANES, :] = product[a * LANES:(a + 1) * LANES, col:col + LANES]


def gram(pieces, places, scale):
    width = pieces[0].shape[1]
    count = len(pieces)
    order = sum(piece.shape[0] for piece in pieces)
    rows = len(upper_blocks(order // LANES)) * LANES
    return pl.pallas_call(
        functools.partial(gram_kernel, scale, count),
        out_shape=jax.ShapeDtypeStruct((rows, LANES), jnp.float32),
        in_specs=[pl.BlockSpec(memory_space=pltpu.SMEM)]
        + [pl.BlockSpec(memory_space=pltpu.VMEM)] * count,
        out_specs=pl.BlockSpec(memory_space=pltpu.VMEM),
        scratch_shapes=[pltpu.VMEM((order, width), jnp.bfloat16)],
        compiler_params=pltpu.CompilerParams(vmem_limit_bytes=40 * 2**20),
        cost_estimate=pl.CostEstimate(
            flops=2 * order * order * width,
            bytes_accessed=2 * order * width + 4 * rows * LANES,
            transcendentals=0,
        ),
        name="gram",
    )(places, *pieces)


CHIPS = ("pair", "dev")


def exchange(x):
    return lax.all_to_all(x, CHIPS, split_axis=0, concat_axis=0, tiled=True)


def swap_cores(x):
    return lax.ppermute(x, "core", [(0, 1), (1, 0)])


def summed_halves(part):
    chips = lax.axis_size(CHIPS)
    core = lax.axis_index("core")
    rows = part.shape[0]
    part = jnp.pad(part, ((0, -rows % (16 * chips)), (0, 0)))
    half = part.shape[0] // 2
    theirs = lax.dynamic_slice_in_dim(part, (1 - core) * half, half)
    mine = lax.dynamic_slice_in_dim(part, core * half, half)
    mine = mine + swap_cores(theirs)
    share = exchange(mine.reshape(chips, half // chips, LANES)).sum(axis=0)
    mine = exchange(jnp.broadcast_to(share[None], (chips, *share.shape))).reshape(half, LANES)
    return mine, swap_cores(mine)


def spread_lane(rows, lane):
    return jnp.broadcast_to(rows[:, lane:lane + 1], rows.shape)


def spread_row(rows, row):
    return jnp.broadcast_to(rows[row:row + 1, :], rows.shape)


def factor_block(block, step):
    lane = lax.broadcasted_iota(jnp.int32, (step, LANES), 1)
    row = lax.broadcasted_iota(jnp.int32, (step, LANES), 0)
    rows = [block[i * step:(i + 1) * step, :] for i in range(LANES // step)]
    tri_rows, inv_rows = [], []
    for t, head in enumerate(rows):
        first = t * step
        inside = (lane >= first) & (lane < first + step)
        spread = [spread_lane(head, first + b) for b in range(step)]
        s = {(a, b): spread_row(spread[b], a) for a in range(step) for b in range(a, step)}
        r, inv_diag = {}, []
        for k in range(step):
            inv = lax.rsqrt(s[k, k])
            inv_diag.append(inv)
            for b in range(k, step):
                r[k, b] = s[k, b] * inv
            for a in range(k + 1, step):
                for b in range(a, step):
                    s[a, b] = s[a, b] - r[k, a] * r[k, b]
        tri, mix = [], []
        for k in range(step):
            raw = spread_row(head, k)
            x = raw
            y = jnp.where(inside, jnp.where(lane == first + k, 1.0, 0.0), raw)
            for m in range(k):
                x = x - r[m, k] * tri[m]
                y = y - r[m, k] * mix[m]
            tri.append(x * inv_diag[k])
            mix.append(y * inv_diag[k])
        tri_out, mix_out = tri[0], mix[0]
        for k in range(1, step):
            tri_out = jnp.where(row == k, tri[k], tri_out)
            mix_out = jnp.where(row == k, mix[k], mix_out)
        tri_rows.append(jnp.where(lane >= row + first, tri_out, 0.0))
        inv_rows.append(jnp.where(lane <= row + first, mix_out, 0.0))
        for i in range(t + 1, LANES // step):
            col, held = [], jnp.where(inside, 0.0, rows[i])
            for k in range(step):
                c = spread_lane(rows[i], first + k)
                for m in range(k):
                    c = c - r[m, k] * col[m]
                col.append(c * inv_diag[k])
                held = held - col[k] * mix[k]
            rows[i] = held
    return tri_rows, inv_rows


def triangle_kernel(count, place_ref, mine_ref, other_ref, out_ref, work_ref, tri_ref, inv_ref):
    step = 8
    high = lax.Precision.HIGHEST
    half = mine_ref.shape[0]
    first_core = place_ref[2] == 0
    order = count * LANES

    def rows(a):
        return slice(a * LANES, (a + 1) * LANES)

    def take_off(p, a, first, last):
        work_ref[rows(a), first:last] -= lax.dot_general(
            tri_ref[rows(p), rows(a)], tri_ref[rows(p), first:last],
            (((0,), (0,)), ((), ())), precision=high, preferred_element_type=jnp.float32,
        )

    for n, (a, b) in enumerate(upper_blocks(count)):
        at = n * LANES % half
        near, far = (mine_ref, other_ref) if n * LANES < half else (other_ref, mine_ref)
        work_ref[rows(a), rows(b)] = jnp.where(first_core, near[at:at + LANES, :], far[at:at + LANES, :])
    tri_ref[...] = jnp.zeros_like(tri_ref)
    for p in range(count):
        tri_rows, inv_rows = factor_block(work_ref[rows(p), rows(p)], step)
        for i in range(LANES // step):
            at = slice(p * LANES + i * step, p * LANES + (i + 1) * step)
            tri_ref[at, rows(p)] = tri_rows[i]
            inv_ref[i * step:(i + 1) * step, :] = inv_rows[i]
        if p + 1 == count:
            break
        after = (p + 1) * LANES
        tri_ref[rows(p), after:] = jnp.dot(
            inv_ref[...], work_ref[rows(p), after:], precision=high, preferred_element_type=jnp.float32
        )
        take_off(p, p + 1, after, after + LANES)
        if after + LANES < order:
            take_off(p, p + 1, after + LANES, order)
        for a in range(p + 2, count):
            take_off(p, a, a * LANES, order)
    out_rows = out_ref.shape[0]
    row = pl.multiple_of(place_ref[0] * out_rows, 8)
    col = pl.multiple_of(place_ref[1] * LANES, LANES)
    out_ref[...] = tri_ref[pl.ds(row, out_rows), pl.ds(col, LANES)]


def own_triangle(mine, other, order):
    row_count = order // lax.axis_size("dev")
    col_count = order // lax.axis_size(GROUP)
    grp = lax.axis_index(GROUP)
    place = [lax.axis_index("dev"), grp * col_count // LANES, lax.axis_index("core")]
    place = jnp.stack(place).astype(jnp.int32)
    count = order // LANES
    out = pl.pallas_call(
        functools.partial(triangle_kernel, count),
        out_shape=jax.ShapeDtypeStruct((row_count, LANES), jnp.float32),
        in_specs=[pl.BlockSpec(memory_space=pltpu.SMEM)] + [pl.BlockSpec(memory_space=pltpu.VMEM)] * 2,
        out_specs=pl.BlockSpec(memory_space=pltpu.VMEM),
        scratch_shapes=[
            pltpu.VMEM((order, order), jnp.float32),
            pltpu.VMEM((order, order), jnp.float32),
            pltpu.VMEM((LANES, LANES), jnp.float32),
        ],
        compiler_params=pltpu.CompilerParams(vmem_limit_bytes=32 * 2**20),
        cost_estimate=pl.CostEstimate(
            flops=order**3, bytes_accessed=4 * order * order, transcendentals=order
        ),
        name="triangle",
    )(place, mine, other)
    if col_count == LANES:
        return out
    return lax.dynamic_slice(out, (0, grp * col_count % LANES), (row_count, col_count))


def per_device(tensor_slab, mode_factor):
    depth, cols, slab_depth, species = tensor_slab.shape
    rank = mode_factor.shape[1]
    n_dev = lax.axis_size("dev")
    n_grp = lax.axis_size(GROUP)
    me = lax.axis_index("dev")
    slab = tensor_slab.transpose(1, 2, 3, 0).reshape(cols, slab_depth * species, depth)
    width = slab_depth * species // n_dev
    factor = mode_factor.T
    pieces, places = [], []
    half = n_dev // 2
    near, far = list(range(1, half)), list(range(half, n_dev))
    order = far[:1] + near[:1] + far[1:2] + near[1:2] + far[2:] + near[2:] + [0]
    for offset in order:
        other = jnp.bitwise_xor(me, offset).astype(jnp.int32)
        cuts = 2 if offset == half and cols % 32 == 0 else 1
        for first in range(0, cols, cols // cuts):
            piece = project(slab, factor, other, width, first, cols // cuts)
            if offset:
                piece = lax.ppermute(piece, "dev", [(i, i ^ offset) for i in range(n_dev)])
            pieces.append(piece)
            places.append(other * cols + first)
    row_total = rank * slab_depth * species * n_grp
    part = gram(pieces, jnp.stack(places), 1.0 / row_total)
    mine, other = summed_halves(part)
    return own_triangle(mine, other, cols * n_dev)


def solution(mesh):
    cores = 2
    devices = mesh.devices
    split = jax.sharding.Mesh(
        devices.reshape(devices.shape[0] // cores, cores, devices.shape[1]), (*GROUP, "dev")
    )
    in_specs = (P(None, "dev", GROUP, None), P())
    out_specs = P("dev", GROUP)
    return jax.shard_map(
        per_device, mesh=split, in_specs=in_specs, out_specs=out_specs, check_vma=False
    )
```
